128 devices in a mesh: group: 16 (over x, z), cuts: 8 (over y, core).
Axes of the slice: x: 4, y: 4, z: 4, core: 2. Of those that a mesh axis runs over, the one named last changes fastest.
Arguments:
- acts: bfloat16 [2048, 6144], P('group', 'cuts'), may hold values from -6 to 6
- grad_out: bfloat16 [2048, 6144], P('group', 'cuts'), may hold values from -6 to 6
- expert_ids: int32 [2048, 2], P('group'), may hold values from 0 to 3, all different within a row; in each aligned block of 128 rows (0 to 127, 128 to 255, ...) at most 80 rows name the same one
- combine: float32 [2048, 2], P('group'), may hold values from 0.1 to 1
- gate_pre: bfloat16 [1280, 65536], P(None, ('group', 'cuts')), may hold values from -6 to 6
- up_weight: bfloat16 [6144, 65536], P(None, ('group', 'cuts')), may hold values from -0.078125 to 0.078125
- down_weight: bfloat16 [65536, 6144], P(('group', 'cuts')), may hold values from -0.046875 to 0.046875
Outputs:
- grad_acts: bfloat16 [2048, 6144], P('group', 'cuts')
- grad_combine: float32 [2048, 2], P('group')
- grad_up: bfloat16 [6144, 65536], P(None, ('group', 'cuts'))
- grad_down: bfloat16 [65536, 6144], P(('group', 'cuts'))
- grad_gate_pre: bfloat16 [1280, 65536], P(None, ('group', 'cuts'))
The draws below stay inside these ranges and needn't reach their ends.
Inputs may be any that keep to these rules, and one draw needn't show every extreme that they name: `expert_ids`: each token names 2 different experts; in each aligned block of 128 tokens no expert is named by more than 80 tokens, a bound that some block reaches.
All inputs are finite; a program needn't handle non-finite values.
Results may differ from the reference program's by a relative error of at most 0.023.
Values may be sent and summed in bfloat16 or wider, within the bound.
No kernel may reach another device: no remote copies, remote signals or barrier semaphores. Data moves between devices by JAX's collectives and lax.ppermute only.
A program may use at most 192 MiB of HBM per device.

```python
import math
import jax
import jax.numpy as jnp
import numpy as np
from jax import lax

D = 6144
EXPERTS = 4
TOP = 2
TOK_G = 128
FF = 16384
MOST = 80
TOKENS = 2048
SLOTS = 1280
N_GROUP = 16


def steps_of(key, extent, shards, least, top_value):
    def one(dim, blocks):
        heights = jax.random.uniform(jax.random.fold_in(jax.random.fold_in(key, 6), dim), (blocks,), jnp.float32, least / len(shards), top_value / len(shards))
        return jnp.repeat(jnp.exp(heights), extent[dim] // blocks).reshape((-1,) + (1,) * (len(extent) - dim - 1))

    level = one(*shards[0])
    for cut in shards[1:]:
        level = level * one(*cut)
    return level


def assign_block(stream_key, own, number, rows, number_of, top, bound, skew):
    sequence = jax.random.permutation(stream_key, number_of)
    crowded, common = portions_of(number_of, rows * top, bound, skew, True), portions_of(number_of, rows * top, bound, skew, False)
    places = jnp.arange(number_of)

    def named(tallies, turn):
        used = int((tallies > 0).sum())
        fixed = max(1, used // 4)
        passed = fixed + (places - fixed + turn * (used - fixed)) % max(1, number_of - fixed)
        return jnp.zeros((number_of,), jnp.int32).at[sequence[jnp.where(places < fixed, places, passed)]].set(jnp.asarray(tallies, jnp.int32))

    tallies = jnp.where(number % 4 == 0, named(crowded, number // 4), named(common, number - number // 4 - 1))
    mixed = jax.random.permutation(jax.random.fold_in(own, 3), number_of)
    source_of, taker = mixed[0:number_of // 2 * 2:2], mixed[1:number_of // 2 * 2:2]
    room = jnp.minimum(tallies[source_of] - 1, bound - tallies[taker]) // 2
    room = jnp.where((source_of == sequence[0]) | (taker == sequence[0]) | (tallies[taker] == 0), 0, jnp.maximum(room, 0))
    passed = jax.random.randint(jax.random.fold_in(own, 4), (number_of // 2,), 0, 1 << 20) % (room + 1)
    tallies = tallies.at[source_of].add(-passed).at[taker].add(passed)
    labels = jnp.searchsorted(jnp.cumsum(tallies), jnp.arange(rows * top), side="right").astype(jnp.int32)
    table = labels.reshape(top, rows).T
    table = table[jax.random.permutation(jax.random.fold_in(own, 1), rows)]
    turn = jax.random.randint(jax.random.fold_in(own, 2), (rows, 1), 0, top)
    return jnp.take_along_axis(table, (jnp.arange(top)[None, :] + turn) % top, axis=1)


def portions_of(number_of, total, limit, skew, full):
    portions = [(1 << 20) // math.isqrt(rank ** skew) + 1 for rank in range(1, number_of + 1)]
    largest = limit if full else min(limit, max(-(-total // number_of), total * portions[0] // sum(portions)))
    least = 1 if total - largest >= number_of - 1 else 0
    holding, surplus = [largest] + [least] * (number_of - 1), total - largest - least * (number_of - 1)
    while surplus > 0:
        candidates = [i for i in range(1, number_of) if holding[i] < largest] or [i for i in range(1, number_of) if holding[i] < limit]
        pool, budget = sum([portions[i] for i in candidates]), surplus
        for i in candidates:
            more = min(limit - holding[i], max(1, budget * portions[i] // pool), surplus)
            holding[i] = holding[i] + more
            surplus = surplus - more
    return np.array(holding)


def normal_values(key, extent, deviation, limit, shards=(), held_as=jnp.bfloat16):
    entries = jax.random.normal(key, extent, jnp.float32) * deviation
    if len(shards) > 0:
        entries = steps_of(key, extent, shards, -0.22, 0.18) * entries
    return jnp.clip(entries, min=-limit, max=limit).astype(held_as)


def setup_inputs(seed: int = 0) -> dict:
    key_list = jax.random.split(jax.random.key(seed), 8)
    acts = normal_values(key_list[0], (TOKENS, D), 1.0, 6.0, ((0, 16), (1, 8)))
    grad_out = normal_values(key_list[1], (TOKENS, D), 1.0, 6.0, ((0, 16), (1, 8)))
    expert_ids_keys = jax.random.split(jax.random.fold_in(key_list[2], 1), TOKENS // TOK_G)
    expert_ids_turns = jax.random.permutation(jax.random.fold_in(key_list[2], 3), TOKENS // TOK_G)
    expert_ids = jax.vmap(lambda own, number: assign_block(jax.random.fold_in(key_list[2], 2), own, number, TOK_G, EXPERTS, TOP, MOST, 2))(expert_ids_keys, expert_ids_turns).reshape((TOKENS, TOP))
    combine = jnp.clip(0.1 + 0.9 * jax.random.uniform(key_list[3], (TOKENS, TOP), jnp.float32) ** steps_of(key_list[3], (TOKENS, TOP), ((0, 16),), -0.2, 0.2), 0.1, 1.0)
    gate_pre = normal_values(key_list[4], (SLOTS, EXPERTS * FF), 1.5, 6.0, ((1, 128),))
    up_weight = normal_values(key_list[5], (D, EXPERTS * FF), D ** -0.5, 0.078125, ((1, 128),))
    down_weight = normal_values(key_list[6], (EXPERTS * FF, D), FF ** -0.5, 0.046875, ((0, 128),))
    return {"acts": acts, "grad_out": grad_out, "expert_ids": expert_ids, "combine": combine, "gate_pre": gate_pre, "up_weight": up_weight, "down_weight": down_weight}


root_coef = math.sqrt(2.0 / math.pi)

def gelu_pair(gate):
    inner = root_coef * (gate + 0.044715 * gate * gate * gate)
    tval = jnp.tanh(inner)
    act = 0.5 * gate * (1.0 + tval)
    slope = 0.5 * (1.0 + tval) + 0.5 * gate * (1.0 - tval * tval) * root_coef * (1.0 + 3.0 * 0.044715 * gate * gate)
    return (act, slope)

def expert_work(slot_acts, slot_grad, slot_weight, gate_slice, up_slice, down_slice):
    upv = jnp.dot(slot_acts, up_slice, preferred_element_type=jnp.float32)
    act, slope = gelu_pair(gate_slice.astype(jnp.float32))
    hidden = (act * upv).astype(jnp.bfloat16)
    raw = lax.dot_general(slot_grad, down_slice, (((1,), (1,)), ((), ())), preferred_element_type=jnp.float32)
    dhid = slot_weight[:, None] * raw
    dup = (dhid * act).astype(jnp.bfloat16)
    grad_gate = (dhid * upv * slope).astype(jnp.bfloat16)
    wgrad = (slot_weight[:, None] * slot_grad.astype(jnp.float32)).astype(jnp.bfloat16)
    grad_up = lax.dot_general(slot_acts, dup, (((0,), (0,)), ((), ())), preferred_element_type=jnp.float32).astype(jnp.bfloat16)
    grad_down = lax.dot_general(hidden, wgrad, (((0,), (0,)), ((), ())), preferred_element_type=jnp.float32).astype(jnp.bfloat16)
    slot_input = lax.dot_general(dup, up_slice, (((1,), (1,)), ((), ())), preferred_element_type=jnp.float32)
    slot_route = lax.optimization_barrier(jnp.sum(hidden.astype(jnp.float32) * raw, axis=1))
    return (slot_input, slot_route, grad_up, grad_down, grad_gate)

def reference(acts, grad_out, expert_ids, combine, gate_pre, up_weight, down_weight):
    high = lax.Precision.HIGHEST
    ids3 = expert_ids.reshape(N_GROUP, TOK_G, TOP)
    comb3 = combine.reshape(N_GROUP, TOK_G, TOP)
    eidx = jnp.arange(EXPERTS, dtype=jnp.int32)
    hit = ids3[..., None] == eidx
    member = jnp.any(hit, axis=2).astype(jnp.int32)
    wtab = lax.optimization_barrier(jnp.sum(comb3[..., None] * hit.astype(jnp.float32), axis=2))
    rank = jnp.cumsum(member, axis=1) - member
    places = jnp.arange(MOST, dtype=jnp.int32)
    member_t = jnp.transpose(member, (0, 2, 1))[:, :, None, :]
    rank_t = jnp.transpose(rank, (0, 2, 1))[:, :, None, :]
    match = ((member_t == 1) & (rank_t == places[None, None, :, None])).astype(jnp.float32)
    acts3 = acts.reshape(N_GROUP, TOK_G, D).astype(jnp.float32)
    grad3 = grad_out.reshape(N_GROUP, TOK_G, D).astype(jnp.float32)
    input_sum = jnp.zeros((N_GROUP, TOK_G, D), jnp.float32)
    route_sum = jnp.zeros((N_GROUP, TOK_G, TOP), jnp.float32)
    ups, downs, gates = ([], [], [])
    for expert in range(EXPERTS):
        onehot = match[:, expert]
        slot_acts = jnp.einsum('spt,std->spd', onehot, acts3, precision=high).reshape(SLOTS, D).astype(jnp.bfloat16)
        slot_grad = jnp.einsum('spt,std->spd', onehot, grad3, precision=high).reshape(SLOTS, D).astype(jnp.bfloat16)
        slot_weight = jnp.einsum('spt,st->sp', onehot, wtab[:, :, expert], precision=high).reshape(SLOTS)
        lo_col = expert * FF
        slot_input, slot_route, grad_up, grad_down, grad_gate = expert_work(slot_acts, slot_grad, slot_weight, gate_pre[:, lo_col:lo_col + FF], up_weight[:, lo_col:lo_col + FF], down_weight[lo_col:lo_col + FF])
        input_sum = input_sum + jnp.einsum('spt,spd->std', onehot, slot_input.reshape(N_GROUP, MOST, D), precision=high)
        route_tok = jnp.einsum('spt,sp->st', onehot, slot_route.reshape(N_GROUP, MOST), precision=high)
        route_sum = route_sum + route_tok[..., None] * hit[..., expert].astype(jnp.float32)
        ups.append(grad_up)
        downs.append(grad_down)
        gates.append(grad_gate)
    grad_acts = input_sum.reshape(TOKENS, D).astype(jnp.bfloat16)
    grad_combine = route_sum.reshape(TOKENS, TOP)
    return (grad_acts, grad_combine, jnp.concatenate(ups, axis=1), jnp.concatenate(downs, axis=0), jnp.concatenate(gates, axis=1))
```

```python
import functools
import math

import jax
import jax.numpy as jnp
from jax import lax
from jax.experimental import pallas as pl
from jax.experimental.pallas import tpu as pltpu
from jax.sharding import Mesh
from jax.sharding import PartitionSpec as P

EXPERTS = 4
MOST = 80
SIDE = 4

bf16 = jnp.bfloat16
f32 = jnp.float32
hold = lax.optimization_barrier
root_coef = math.sqrt(2.0 / math.pi)


def gelu_pair(gate):
    inner = root_coef * (gate + 0.044715 * gate * gate * gate)
    tval = jnp.tanh(inner)
    act = 0.5 * gate * (1.0 + tval)
    slope = 0.5 * (1.0 + tval) + 0.5 * gate * (1.0 - tval * tval) * root_coef * (
        1.0 + 3.0 * 0.044715 * gate * gate
    )
    return (act, slope)


def go(v, axis, step):
    return lax.ppermute(v, axis, [(i, (i + step) % SIDE) for i in range(SIDE)])


def both(v, axis):
    return go(v, axis, 1), go(v, axis, -1)


def swap(v):
    return lax.ppermute(v, "c", [(0, 1), (1, 0)])


def add(*parts):
    total = parts[0].astype(f32)
    for part in parts[1:]:
        total = total + part.astype(f32)
    return total.astype(bf16)


def gather_1(a, g):
    return both(a, "z") + both(g, "y")


def gather_2(one):
    al, ar, gl, gr = one
    h = al.shape[1] // 2
    return (
        go(al[:, :h], "z", 1),
        go(ar[:, h:], "z", -1),
        go(gl[:, :h], "y", 1),
        go(gr[:, h:], "y", -1),
    )


def gather_join(a, g, one, two):
    al, ar, gl, gr = one
    aa, ab, ga, gb = two
    s = jnp.concatenate([a, al, ar, jnp.concatenate([aa, ab], axis=1)], axis=0)
    t = jnp.concatenate([g, gl, gr, ga, gb], axis=1)
    return s, t


def gather_3(s, t):
    return both(s, "y") + both(t, "z")


def gather_4(three):
    sl, sr, tl, tr = three
    h, w = sl.shape[0] // 2, tl.shape[1] // 2
    return (
        go(sl[:h], "y", 1),
        go(sr[h:], "y", -1),
        go(tl[:, :w], "z", 1),
        go(tr[:, w:], "z", -1),
    )


def ring_sum(own, left, right, opp, axis, along):
    half = opp.shape[along] // 2

    def cut(v):
        return (v[:half], v[half:]) if along == 0 else (v[:, :half], v[:, half:])

    oa, ob = cut(opp)
    ra, rb = hold((go(oa, axis, 1), go(ob, axis, -1)))
    ca, cb = cut(right)
    da, db = cut(left)
    sa = jnp.concatenate([add(ca, ra), cb], axis=along)
    sb = jnp.concatenate([da, add(db, rb)], axis=along)
    fa, fb = go(sa, axis, 1), go(sb, axis, -1)
    return add(own, fa, fb)


def plane_sum(mine, other):
    got = swap(other)
    rows, cols = mine.shape
    n, k = rows // SIDE, cols // 2
    w = k // SIDE

    def part(r0, r1, c0, c1):
        return add(mine[r0:r1, c0:c1], got[r0:r1, c0:c1])

    z_blocks = [part(i * n, (i + 1) * n, 0, k) for i in range(SIDE)]
    y_blocks = [part(0, rows, k + i * w, k + (i + 1) * w) for i in range(SIDE)]
    one = ring_sum(*z_blocks, "z", 1)
    two = ring_sum(*y_blocks, "y", 0)
    one, two = hold((one, two))
    one = ring_sum(*[one[:, i * w : (i + 1) * w] for i in range(SIDE)], "y", 0)
    two = ring_sum(*[two[i * n : (i + 1) * n] for i in range(SIDE)], "z", 0)
    return jnp.concatenate([one, two], axis=1)


def expert_kernel(*refs, first, rows, wide, deep):
    tab = refs[0]
    pieces = refs[1:21]
    gate, up, down = refs[21:24]
    k = 24 if first else 25
    acts_o, wg_o, dup_o, hid_o, mine_o, other_o, gg_o = refs[k : k + 7]
    (a_v, g_v, v_v, w_v, gate_v, o_v, gg_v, dup_v, hid_v, up_acc, raw_acc) = refs[k + 7 : k + 18]
    s_a, s_g, s_v, s_w, s_gate, s_o, s_gg, s_out = refs[k + 18 :]
    n = rows // SIDE
    blk = wide // 8
    half = wide // 2
    copy = pltpu.make_async_copy

    def acts_copies(ci):
        s, sl, sr, sa, sb = pieces[ci * 10 : ci * 10 + 5]
        c0 = ci * half
        dst = [
            (s, 0, rows, 0),
            (sl, 0, rows, 1),
            (sr, 0, rows, 2),
            (sa, 0, rows // 2, 3),
            (sb, rows // 2, rows // 2, 3),
        ]
        return [
            copy(src, a_v.at[pl.ds(r0, m), pl.ds(c0 + q * blk, blk)], s_a.at[ci * 5 + i])
            for i, (src, r0, m, q) in enumerate(dst)
        ]

    def grad_copies(ci):
        t, tl, tr, ta, tb = pieces[ci * 10 + 5 : ci * 10 + 10]
        c0 = ci * half
        dst = [
            (t, 0, 0, half),
            (tl, 1, 0, half),
            (tr, 2, 0, half),
            (ta, 3, 0, half // 2),
            (tb, 3, half // 2, half // 2),
        ]
        return [
            copy(src, g_v.at[pl.ds(z * n, n), pl.ds(c0 + c, m)], s_g.at[ci * 5 + i])
            for i, (src, z, c, m) in enumerate(dst)
        ]

    def place(q):
        return pl.multiple_of(tab[q] * blk, blk)

    v_copies = [
        copy(up.at[pl.ds(place(q), blk)], v_v.at[pl.ds(q * blk, blk)], s_v.at[q]) for q in range(8)
    ]
    w_copies = [
        copy(down.at[:, pl.ds(place(q), blk)], w_v.at[:, pl.ds(q * blk, blk)], s_w.at[q])
        for q in range(8)
    ]

    def gate_row(i):
        return pl.multiple_of(tab[8 + i] * MOST, MOST)

    gate_copies = [
        copy(gate.at[pl.ds(gate_row(i), MOST)], gate_v.at[pl.ds(i * MOST, MOST)], s_gate.at[i])
        for i in range(8)
    ]
    gg_copies = [
        copy(gg_v.at[pl.ds(i * MOST, MOST)], gg_o.at[pl.ds(gate_row(i), MOST)], s_gg.at[i])
        for i in range(8)
    ]
    a_in = [acts_copies(0), acts_copies(1)]
    g_in = [grad_copies(0), grad_copies(1)]
    for ci in range(2):
        for i in range(5):
            a_in[ci][i].start()
            if i < 4:
                v_copies[ci * 4 + i].start()
    for ci in range(2):
        for i in range(5):
            g_in[ci][i].start()
            if i < 4:
                w_copies[ci * 4 + i].start()
    for cp in gate_copies:
        cp.start()

    for q in range(8):
        ci, i = divmod(q, 4)
        a_in[ci][i].wait()
        if i == 3:
            a_in[ci][4].wait()
        v_copies[q].wait()
        part = jnp.dot(
            a_v[:, q * blk : (q + 1) * blk],
            v_v[q * blk : (q + 1) * blk, :],
            preferred_element_type=f32,
        )
        if q == 0:
            up_acc[...] = part
        else:
            up_acc[...] += part
    acts_out = copy(a_v, acts_o, s_out.at[0])
    acts_out.start()
    for q in range(8):
        ci, i = divmod(q, 4)
        if i == 0:
            for cp in g_in[ci]:
                cp.wait()
        w_copies[q].wait()
        part = lax.dot_general(
            g_v[:, q * blk : (q + 1) * blk],
            w_v[:, q * blk : (q + 1) * blk],
            (((1,), (1,)), ((), ())),
            preferred_element_type=f32,
        )
        if q == 0:
            raw_acc[...] = part
        else:
            raw_acc[...] += part
    wg_out = copy(g_v, wg_o, s_out.at[1])
    wg_out.start()
    for cp in gate_copies:
        cp.wait()

    def middle(i, carry):
        at = pl.ds(pl.multiple_of(i * MOST, MOST), MOST)
        act, slope = gelu_pair(gate_v[at, :].astype(f32))
        upv = up_acc[at, :]
        dhid = raw_acc[at, :]
        hid_v[at, :] = (act * upv).astype(bf16)
        dup_v[at, :] = (dhid * act).astype(bf16)
        gg_v[at, :] = (dhid * upv * slope).astype(bf16)
        return carry

    lax.fori_loop(0, rows // MOST, middle, 0)
    for cp in gg_copies:
        cp.start()
    hid_out = copy(hid_v, hid_o, s_out.at[2])
    dup_out = copy(dup_v, dup_o, s_out.at[3])
    hid_out.start()
    dup_out.start()

    flying = [None, None]
    for turn, q in enumerate((4, 5, 6, 7, 0, 1, 2, 3)):
        slot = turn % 2
        if flying[slot] is not None:
            for cp in flying[slot]:
                cp.wait()
        o_v[slot] = lax.dot_general(
            dup_v[...],
            v_v[q * blk : (q + 1) * blk, :],
            (((1,), (1,)), ((), ())),
            preferred_element_type=f32,
        ).astype(bf16)
        out = other_o if q >= 4 else mine_o
        r, w = q % 4, blk // 2
        flying[slot] = [
            copy(
                o_v.at[slot, :, pl.ds(h * w, w)],
                out.at[:, pl.ds(h * (half // 2) + r * w, w)],
                s_o.at[slot * 2 + h],
            )
            for h in range(2)
        ]
        for cp in flying[slot]:
            cp.start()
    for pair in flying:
        for cp in pair:
            cp.wait()
    for cp in gg_copies:
        cp.wait()
    for cp in (acts_out, wg_out, hid_out, dup_out):
        cp.wait()


def expert_call(tab, pieces, gate, up, down, gg):
    wide, deep = up.shape
    rows = pieces[0].shape[0]
    first = gg is None
    anyspec = pl.BlockSpec(memory_space=pl.ANY)
    sds = jax.ShapeDtypeStruct
    ins = [tab, *pieces, gate, up, down] + ([] if first else [gg])
    dma = pltpu.SemaphoreType.DMA
    return pl.pallas_call(
        functools.partial(expert_kernel, first=first, rows=rows, wide=wide, deep=deep),
        out_shape=(
            sds((rows, wide), bf16),
            sds((rows, wide), bf16),
            sds((rows, deep), bf16),
            sds((rows, deep), bf16),
            sds((rows, wide // 2), bf16),
            sds((rows, wide // 2), bf16),
            sds(gate.shape, bf16),
        ),
        in_specs=[pl.BlockSpec(memory_space=pltpu.SMEM)] + [anyspec] * (len(ins) - 1),
        out_specs=(anyspec,) * 7,
        scratch_shapes=[
            pltpu.VMEM((rows, wide), bf16),
            pltpu.VMEM((rows, wide), bf16),
            pltpu.VMEM((wide, deep), bf16),
            pltpu.VMEM((deep, wide), bf16),
            pltpu.VMEM((rows, deep), bf16),
            pltpu.VMEM((2, rows, wide // 8), bf16),
            pltpu.VMEM((rows, deep), bf16),
            pltpu.VMEM((rows, deep), bf16),
            pltpu.VMEM((rows, deep), bf16),
            pltpu.VMEM((rows, deep), f32),
            pltpu.VMEM((rows, deep), f32),
            dma((10,)),
            dma((10,)),
            dma((8,)),
            dma((8,)),
            dma((8,)),
            dma((4,)),
            dma((8,)),
            dma((4,)),
        ],
        input_output_aliases={} if first else {len(ins) - 1: 6},
        compiler_params=pltpu.CompilerParams(vmem_limit_bytes=56 * 2**20),
        cost_estimate=pl.CostEstimate(
            flops=6 * rows * wide * deep, bytes_accessed=2 * (5 * rows * wide), transcendentals=0
        ),
        name="expert_rows",
    )(*ins)


def up_grad_kernel(tab, a0, a1, d0, d1, out):
    def dot(a, d):
        return lax.dot_general(
            a[...], d[...], (((0,), (0,)), ((), ())), preferred_element_type=f32
        )

    out[...] = (dot(a0, d0) + dot(a1, d1)).astype(bf16)


def up_grad_call(tab, a0, a1, d0, d1):
    rows, wide = a0.shape
    deep = d0.shape[1]
    blk = wide // 8
    left = pl.BlockSpec((rows, blk), lambda q, tab: (0, q))
    right = pl.BlockSpec((rows, deep), lambda q, tab: (0, 0))
    return pl.pallas_call(
        up_grad_kernel,
        out_shape=jax.ShapeDtypeStruct((wide, deep), bf16),
        grid_spec=pltpu.PrefetchScalarGridSpec(
            num_scalar_prefetch=1,
            grid=(8,),
            in_specs=[left, left, right, right],
            out_specs=pl.BlockSpec((blk, deep), lambda q, tab: (tab[q], 0)),
        ),
        compiler_params=pltpu.CompilerParams(vmem_limit_bytes=40 * 2**20),
        cost_estimate=pl.CostEstimate(
            flops=4 * rows * wide * deep, bytes_accessed=4 * rows * wide, transcendentals=0
        ),
        name="up_grad",
    )(tab, a0, a1, d0, d1)


def down_grad_call(tab, g0, g1, h0, h1):
    rows, wide = g0.shape
    deep = h0.shape[1]
    blk = wide // 8
    right = pl.BlockSpec((rows, blk), lambda q, tab: (0, q))
    left = pl.BlockSpec((rows, deep), lambda q, tab: (0, 0))

    def kernel(tab, g0, g1, h0, h1, out):
        def dot(h, g):
            return lax.dot_general(
                h[...], g[...], (((0,), (0,)), ((), ())), preferred_element_type=f32
            )

        out[...] = (dot(h0, g0) + dot(h1, g1)).astype(bf16)

    return pl.pallas_call(
        kernel,
        out_shape=jax.ShapeDtypeStruct((deep, wide), bf16),
        grid_spec=pltpu.PrefetchScalarGridSpec(
            num_scalar_prefetch=1,
            grid=(8,),
            in_specs=[right, right, left, left],
            out_specs=pl.BlockSpec((deep, blk), lambda q, tab: (0, tab[q])),
        ),
        compiler_params=pltpu.CompilerParams(vmem_limit_bytes=40 * 2**20),
        cost_estimate=pl.CostEstimate(
            flops=4 * rows * wide * deep, bytes_accessed=4 * rows * wide, transcendentals=0
        ),
        name="down_grad",
    )(tab, g0, g1, h0, h1)


def body(acts, grad_out, expert_ids, combine, gate_pre, up_weight, down_weight):
    x, z, y, c = (lax.axis_index(name) for name in ("x", "z", "y", "c"))
    rel = jnp.arange(EXPERTS, dtype=jnp.int32)
    hit = expert_ids[:, :, None] == (x + rel) % EXPERTS
    member = jnp.any(hit, axis=1)
    wtab = jnp.sum(combine[:, :, None] * hit.astype(f32), axis=1)
    count = member.astype(jnp.int32)
    rank = jnp.cumsum(count, axis=0) - count
    places = jnp.arange(MOST, dtype=jnp.int32)
    found = member.T[:, None, :] & (rank.T[:, None, :] == places[None, :, None])
    match = found.astype(bf16).reshape(EXPERTS * MOST, -1)
    weight = jnp.sum(found.astype(f32) * wtab.T[:, None, :], axis=2).reshape(-1)
    used = jnp.any(found, axis=2).reshape(-1)

    slot_acts = jnp.dot(match, acts, preferred_element_type=f32).astype(bf16)
    slot_grad = jnp.dot(match, grad_out, preferred_element_type=f32)
    slot_wgrad = (weight[:, None] * slot_grad).astype(bf16)

    def send(k, step):
        rows = slice(k * MOST, (k + 1) * MOST)
        return go(jnp.concatenate([slot_acts[rows], slot_wgrad[rows]], axis=0), "x", step)

    back_1 = send(1, 1)
    back_3 = send(3, -1)
    back_2 = send(2, 2)
    a0 = jnp.concatenate([slot_acts[:MOST], back_1[:MOST]], axis=0)
    g0 = jnp.concatenate([slot_wgrad[:MOST], back_1[MOST:]], axis=0)
    a1 = jnp.concatenate([back_3[:MOST], back_2[:MOST]], axis=0)
    g1 = jnp.concatenate([back_3[MOST:], back_2[MOST:]], axis=0)

    ring = jnp.array([0, SIDE - 1, 1, 2], jnp.int32)
    ys, zs = (y + ring) % SIDE, (z + ring) % SIDE
    cols = jnp.concatenate([ys * 2 + c, ys * 2 + 1 - c])

    def table(d0, d1):
        xs = (x + jnp.array([d0, d1], jnp.int32)) % SIDE
        return jnp.concatenate([cols, (xs[None, :] * SIDE + zs[:, None]).reshape(-1)]).astype(
            jnp.int32
        )

    tab0, tab1 = table(0, 3), table(1, 2)

    one0 = gather_1(a0, g0)
    one0, a1, g1 = hold((one0, a1, g1))
    two0 = gather_2(one0)
    one1 = gather_1(a1, g1)
    two0, one1 = hold((two0, one1))
    s0, t0 = gather_join(a0, g0, one0, two0)
    three0 = gather_3(s0, t0)
    two1 = gather_2(one1)
    three0, two1 = hold((three0, two1))
    own0 = (s0, t0) + three0
    four0 = gather_4(three0)
    s1, t1 = gather_join(a1, g1, one1, two1)
    three1 = gather_3(s1, t1)
    four1 = gather_4(three1)

    def pieces(s, t, three, four):
        sl, sr, tl, tr = three
        sa, sb, ta, tb = four
        own = [s, sl, sr, sa, sb, t, tl, tr, ta, tb]
        return own + [swap(v) for v in own]

    e0 = expert_call(tab0, pieces(s0, t0, three0, four0), gate_pre, up_weight, down_weight, None)
    acts0, wg0, dup0, hid0, mine0, other0, gg = e0
    e1 = expert_call(tab1, pieces(s1, t1, three1, four1), gate_pre, up_weight, down_weight, gg)
    acts1, wg1, dup1, hid1, mine1, other1, gg = e1

    sum0 = plane_sum(mine0, other0)
    sum1 = plane_sum(mine1, other1)
    grad_up = up_grad_call(tab0, acts0, acts1, dup0, dup1)
    grad_down = down_grad_call(tab0, wg0, wg1, hid0, hid1)

    home = jnp.concatenate(
        [sum0[:MOST], go(sum0[MOST:], "x", -1), go(sum1[MOST:], "x", 2), go(sum1[:MOST], "x", 1)],
        axis=0,
    )
    own_input = lax.dot_general(
        match, home, (((0,), (0,)), ((), ())), preferred_element_type=f32
    ).astype(bf16)
    route = jnp.sum(home.astype(f32) * slot_acts.astype(f32), axis=1)
    route = jnp.where(used, route / jnp.where(used, weight, 1.0), 0.0).reshape(EXPERTS, MOST)
    token_route = jnp.sum(found.astype(f32) * route[:, :, None], axis=1).T
    terms = jnp.sum(token_route[:, None, :] * hit.astype(f32), axis=2)
    terms = terms + swap(terms)
    terms = (terms + go(terms, "y", 2)) + (go(terms, "y", 1) + go(terms, "y", -1))
    return (own_input, terms, grad_up, grad_down, gg)


def solution(mesh):
    grid = Mesh(mesh.devices.reshape(SIDE, SIDE, SIDE, 2), ("x", "z", "y", "c"))
    group, cuts, every = ("x", "z"), ("y", "c"), ("x", "z", "y", "c")
    return jax.shard_map(
        body,
        mesh=grid,
        in_specs=(
            P(group, cuts),
            P(group, cuts),
            P(group, None),
            P(group, None),
            P(None, every),
            P(None, every),
            P(every, None),
        ),
        out_specs=(
            P(group, cuts),
            P(group, None),
            P(None, every),
            P(every, None),
            P(None, every),
        ),
        check_vma=False,
    )
```

```python
import functools
import math

import jax
import jax.numpy as jnp
from jax import lax
from jax.experimental import pallas as pl
from jax.experimental.pallas import tpu as pltpu
from jax.sharding import Mesh
from jax.sharding import PartitionSpec as P

EXPERTS = 4
MOST = 80
SIDE = 4

bf16 = jnp.bfloat16
f32 = jnp.float32
hold = lax.optimization_barrier
root_coef = math.sqrt(2.0 / math.pi)


def gelu_pair(gate):
    inner = root_coef * (gate + 0.044715 * gate * gate * gate)
    tval = jnp.tanh(inner)
    act = 0.5 * gate * (1.0 + tval)
    slope = 0.5 * (1.0 + tval) + 0.5 * gate * (1.0 - tval * tval) * root_coef * (
        1.0 + 3.0 * 0.044715 * gate * gate
    )
    return (act, slope)


def go(v, axis, step):
    return lax.ppermute(v, axis, [(i, (i + step) % SIDE) for i in range(SIDE)])


def both(v, axis):
    return go(v, axis, 1), go(v, axis, -1)


def swap(v):
    return lax.ppermute(v, "c", [(0, 1), (1, 0)])


def add(*parts):
    total = parts[0].astype(f32)
    for part in parts[1:]:
        total = total + part.astype(f32)
    return total.astype(bf16)


def ring_far(left, right, axis):
    w = left.shape[1] // 2
    return go(left[:, :w], axis, 1), go(right[:, w:], axis, -1)


def join_rows(a, near, far):
    return jnp.concatenate([a, *near, jnp.concatenate(far, axis=1)], axis=0)


def join_cols(g, near, far):
    return jnp.concatenate([g, *near, *far], axis=1)


def cut(v, along):
    half = v.shape[along] // 2
    return (v[:half], v[half:]) if along == 0 else (v[:, :half], v[:, half:])


def widen(v, along, second):
    pads = [(0, 0), (0, 0)]
    pads[along] = (v.shape[along], 0) if second else (0, v.shape[along])
    return jnp.pad(v, pads)


def ring_all(own, left, right, opp, axis):
    return add(own, go(left, axis, -1), go(right, axis, 1), go(opp, axis, 2))


class PlaneSum:
    def __init__(self, mine, got):
        rows, cols = mine.shape
        self.n, k = rows // SIDE, cols // 2
        self.w = k // SIDE
        n, w = self.n, self.w

        def part(r0, r1, c0, c1):
            return mine[r0:r1, c0:c1], got[r0:r1, c0:c1]

        self.z = [part(i * n, (i + 1) * n, 0, k) for i in range(SIDE)]
        self.y = [part(0, rows, k + i * w, k + (i + 1) * w) for i in range(SIDE)]

    def first(self):
        za, zb = cut(add(*self.z[3]), 1)
        ya, yb = cut(add(*self.y[3]), 0)
        return go(za, "z", 1), go(zb, "z", -1), go(ya, "y", 1), go(yb, "y", -1)

    def second(self, met):
        za, zb, ya, yb = met
        return (
            go(add(*self.z[2], widen(za, 1, False)), "z", 1),
            go(add(*self.z[1], widen(zb, 1, True)), "z", -1),
            go(add(*self.y[2], widen(ya, 0, False)), "y", 1),
            go(add(*self.y[1], widen(yb, 0, True)), "y", -1),
        )

    def third(self, met):
        n, w = self.n, self.w
        one, two = add(*self.z[0], *met[:2]), add(*self.y[0], *met[2:])
        one = ring_all(*[one[:, i * w : (i + 1) * w] for i in range(SIDE)], "y")
        two = ring_all(*[two[i * n : (i + 1) * n] for i in range(SIDE)], "z")
        return jnp.concatenate([one, two], axis=1)


anyspec = pl.BlockSpec(memory_space=pl.ANY)
smem = pl.BlockSpec(memory_space=pltpu.SMEM)
dma = pltpu.SemaphoreType.DMA
sds = jax.ShapeDtypeStruct
NT = (((1,), (1,)), ((), ()))
TN = (((0,), (0,)), ((), ()))


def mul(a, b, dims):
    return lax.dot_general(a, b, dims, preferred_element_type=f32)


def params():
    return pltpu.CompilerParams(vmem_limit_bytes=56 * 2**20)


def cost(flops, moved):
    return pl.CostEstimate(flops=flops, bytes_accessed=moved, transcendentals=0)


def raw_kernel(tab, *refs):
    pieces, down = refs[:10], refs[10]
    raw_o, wg_o, g_v, w_v, raw_acc, s_g, s_w, s_o = refs[11:]
    copy = pltpu.make_async_copy
    n, half = pieces[0].shape
    blk = half // 4

    def grad_copies(ci):
        dst = [(0, 0, half), (1, 0, half), (2, 0, half), (3, 0, half // 2), (3, half // 2, half // 2)]
        return [
            copy(src, g_v.at[pl.ds(z * n, n), pl.ds(ci * half + c, m)], s_g.at[ci * 5 + i])
            for i, (src, (z, c, m)) in enumerate(zip(pieces[ci * 5 : ci * 5 + 5], dst))
        ]

    g_in = [grad_copies(0), grad_copies(1)]
    w_in = [
        copy(down.at[:, pl.ds(pl.multiple_of(tab[q] * blk, blk), blk)], w_v.at[q], s_w.at[q])
        for q in range(8)
    ]
    for ci in range(2):
        for cp in g_in[ci]:
            cp.start()
        for q in range(4):
            w_in[ci * 4 + q].start()
    last = [
        copy(g_v.at[:, pl.ds(ci * half, half)], wg_o.at[:, pl.ds(ci * half, half)], s_o.at[ci])
        for ci in range(2)
    ]
    for q in range(8):
        if q % 4 == 0:
            for cp in g_in[q // 4]:
                cp.wait()
            last[q // 4].start()
        w_in[q].wait()
        part = mul(g_v[:, q * blk : (q + 1) * blk], w_v[q], NT)
        if q == 0:
            raw_acc[...] = part
        else:
            raw_acc[...] += part
    last.append(copy(raw_acc, raw_o, s_o.at[2]))
    last[2].start()
    for cp in last:
        cp.wait()


def raw_call(tab, pieces, down):
    deep, wide = down.shape
    n = pieces[0].shape[0]
    rows = SIDE * n
    return pl.pallas_call(
        raw_kernel,
        out_shape=(sds((rows, deep), f32), sds((rows, wide), bf16)),
        in_specs=[smem] + [anyspec] * 11,
        out_specs=(anyspec,) * 2,
        scratch_shapes=[
            pltpu.VMEM((rows, wide), bf16),
            pltpu.VMEM((8, deep, wide // 8), bf16),
            pltpu.VMEM((rows, deep), f32),
            dma((10,)),
            dma((8,)),
            dma((3,)),
        ],
        compiler_params=params(),
        cost_estimate=cost(2 * rows * wide * deep, 2 * (2 * rows * wide + wide * deep)),
        name="raw_rows",
    )(tab, *pieces, down)


def main_kernel(*refs, first, whole):
    tab, acts, raw, gate, up = refs[:5]
    k = 5 if first else 6
    dup_o, hid_o, gg_o = refs[k : k + 3]
    outs = refs[k + 3 : k + 4] if whole else refs[k + 3 : k + 5]
    k += 4 if whole else 5
    a_v, v_v, gate_v, up_acc, raw_v, dup_v, hid_v, gg_v, o_v = refs[k : k + 9]
    s_a, s_v, s_gate, s_raw, s_gg, s_out, s_o = refs[k + 9 :]
    copy = pltpu.make_async_copy
    rows, blk = a_v.shape[1:]
    n, w = rows // SIDE, blk // 2

    a_in = [copy(acts.at[q], a_v.at[q], s_a.at[q]) for q in range(8)]
    v_in = [copy(up.at[pl.ds(q * blk, blk)], v_v.at[q], s_v.at[q]) for q in range(8)]
    raw_in = copy(raw, raw_v, s_raw.at[0])

    def gate_spot(i):
        return pl.ds(pl.multiple_of(tab[8 + i] * MOST, MOST), MOST)

    gate_in = [
        copy(gate.at[gate_spot(i)], gate_v.at[pl.ds(i * MOST, MOST)], s_gate.at[i])
        for i in range(8)
    ]
    gg_out = [
        copy(gg_v.at[pl.ds(i * MOST, MOST)], gg_o.at[gate_spot(i)], s_gg.at[i]) for i in range(8)
    ]
    for q in range(8):
        a_in[q].start()
        v_in[q].start()
    raw_in.start()
    for cp in gate_in:
        cp.start()
    for q in range(8):
        a_in[q].wait()
        v_in[q].wait()
        part = jnp.dot(a_v[q], v_v[q], preferred_element_type=f32)
        if q == 0:
            up_acc[...] = part
        else:
            up_acc[...] += part
    raw_in.wait()
    for cp in gate_in:
        cp.wait()

    def middle(i, carry):
        at = pl.ds(pl.multiple_of(i * MOST, MOST), MOST)
        act, slope = gelu_pair(gate_v[at, :].astype(f32))
        upv = up_acc[at, :]
        dhid = raw_v[at, :]
        hid_v[at, :] = (act * upv).astype(bf16)
        dup_v[at, :] = (dhid * act).astype(bf16)
        gg_v[at, :] = (dhid * upv * slope).astype(bf16)
        return carry

    lax.fori_loop(0, rows // MOST, middle, 0)
    side = gg_out + [copy(dup_v, dup_o, s_out.at[0]), copy(hid_v, hid_o, s_out.at[1])]
    for cp in side:
        cp.start()

    flying = [[], []]
    for turn, q in enumerate((4, 5, 6, 7, 0, 1, 2, 3)):
        slot = turn % 2
        for cp in flying[slot]:
            cp.wait()
        spot = tab[q]
        o_v[slot] = mul(dup_v[...], v_v[spot], NT).astype(bf16)
        if whole:
            flying[slot] = [
                copy(
                    o_v.at[slot, pl.ds(i * n, n)],
                    outs[0].at[pl.ds(pl.multiple_of((spot * SIDE + tab[16 + i]) * n, n), n)],
                    s_o.at[slot, i],
                )
                for i in range(SIDE)
            ]
        else:
            flying[slot] = [
                copy(
                    o_v.at[slot, :, pl.ds(h * w, w)],
                    outs[0 if q < 4 else 1].at[:, pl.ds(h * 4 * w + q % 4 * w, w)],
                    s_o.at[slot, h],
                )
                for h in range(2)
            ]
        for cp in flying[slot]:
            cp.start()
    for cp in flying[0] + flying[1] + side:
        cp.wait()


def main_call(tab, acts, raw, gate, up, gg, whole):
    wide, deep = up.shape
    rows, blk = acts.shape[1:]
    first = gg is None
    ins = [tab, acts, raw, gate, up] + ([] if first else [gg])
    sums = (
        (sds((rows * 8, blk), bf16),)
        if whole
        else (sds((rows, wide // 2), bf16), sds((rows, wide // 2), bf16))
    )
    return pl.pallas_call(
        functools.partial(main_kernel, first=first, whole=whole),
        out_shape=(sds((rows, deep), bf16), sds((rows, deep), bf16), sds(gate.shape, bf16)) + sums,
        in_specs=[smem] + [anyspec] * (len(ins) - 1),
        out_specs=(anyspec,) * (3 + len(sums)),
        scratch_shapes=[
            pltpu.VMEM((8, rows, blk), bf16),
            pltpu.VMEM((8, blk, deep), bf16),
            pltpu.VMEM((rows, deep), bf16),
            pltpu.VMEM((rows, deep), f32),
            pltpu.VMEM((rows, deep), f32),
            pltpu.VMEM((rows, deep), bf16),
            pltpu.VMEM((rows, deep), bf16),
            pltpu.VMEM((rows, deep), bf16),
            pltpu.VMEM((2, rows, blk), bf16),
            dma((8,)),
            dma((8,)),
            dma((8,)),
            dma((1,)),
            dma((8,)),
            dma((2,)),
            dma((2, 4)),
        ],
        input_output_aliases={} if first else {len(ins) - 1: 2},
        compiler_params=params(),
        cost_estimate=cost(4 * rows * wide * deep, 2 * (2 * rows * wide + wide * deep)),
        name="main_rows",
    )(*ins)


def up_grad_call(a0, a1, d0, d1, part, into):
    rows, blk = a0.shape[1:]
    deep = d0.shape[1]
    left = pl.BlockSpec((None, rows, blk), lambda q: (part * 4 + q, 0, 0))
    right = pl.BlockSpec((rows, deep), lambda q: (0, 0))

    def kernel(a0, a1, d0, d1, *rest):
        out = rest[-1]
        out[...] = (mul(a0[...], d0[...], TN) + mul(a1[...], d1[...], TN)).astype(bf16)

    more = () if into is None else (into,)
    return pl.pallas_call(
        kernel,
        out_shape=sds((8 * blk, deep), bf16),
        grid=(4,),
        in_specs=[left, left, right, right] + [anyspec] * len(more),
        out_specs=pl.BlockSpec((blk, deep), lambda q: (part * 4 + q, 0)),
        input_output_aliases={4: 0} if more else {},
        compiler_params=params(),
        cost_estimate=cost(rows * 8 * blk * deep * 2, 2 * rows * 8 * blk),
        name="up_grad",
    )(a0, a1, d0, d1, *more)


def down_grad_call(tab, g0, g1, h0, h1):
    rows, wide = g0.shape
    deep = h0.shape[1]
    blk = wide // 8
    right = pl.BlockSpec((rows, blk), lambda q, tab: (0, q))
    left = pl.BlockSpec((rows, deep), lambda q, tab: (0, 0))

    def kernel(tab, g0, g1, h0, h1, out):
        out[...] = (mul(h0[...], g0[...], TN) + mul(h1[...], g1[...], TN)).astype(bf16)

    return pl.pallas_call(
        kernel,
        out_shape=sds((deep, wide), bf16),
        grid_spec=pltpu.PrefetchScalarGridSpec(
            num_scalar_prefetch=1,
            grid=(8,),
            in_specs=[right, right, left, left],
            out_specs=pl.BlockSpec((deep, blk), lambda q, tab: (0, tab[q])),
        ),
        compiler_params=params(),
        cost_estimate=cost(rows * wide * deep * 4, 4 * rows * wide),
        name="down_grad",
    )(tab, g0, g1, h0, h1)


def body(acts, grad_out, expert_ids, combine, gate_pre, up_weight, down_weight):
    x, z, y, c = (lax.axis_index(name) for name in ("x", "z", "y", "c"))
    rel = jnp.arange(EXPERTS, dtype=jnp.int32)
    hit = expert_ids[:, :, None] == (x + rel) % EXPERTS
    member = jnp.any(hit, axis=1)
    wtab = jnp.sum(combine[:, :, None] * hit.astype(f32), axis=1)
    count = member.astype(jnp.int32)
    rank = jnp.cumsum(count, axis=0) - count
    places = jnp.arange(MOST, dtype=jnp.int32)
    found = member.T[:, None, :] & (rank.T[:, None, :] == places[None, :, None])
    match = found.astype(bf16).reshape(EXPERTS * MOST, -1)
    weight = jnp.sum(found.astype(f32) * wtab.T[:, None, :], axis=2).reshape(-1)
    used = jnp.any(found, axis=2).reshape(-1)

    slot_acts = jnp.dot(match, acts, preferred_element_type=f32).astype(bf16)
    slot_grad = jnp.dot(match, grad_out, preferred_element_type=f32)
    slot_wgrad = (weight[:, None] * slot_grad).astype(bf16)

    def send(k, step):
        rows = slice(k * MOST, (k + 1) * MOST)
        return go(jnp.concatenate([slot_acts[rows], slot_wgrad[rows]], axis=0), "x", step)

    back_1 = send(1, 1)
    back_3 = send(3, -1)
    back_2 = send(2, 2)
    a0 = jnp.concatenate([slot_acts[:MOST], back_1[:MOST]], axis=0)
    g0 = jnp.concatenate([slot_wgrad[:MOST], back_1[MOST:]], axis=0)
    a1 = jnp.concatenate([back_3[:MOST], back_2[:MOST]], axis=0)
    g1 = jnp.concatenate([back_3[MOST:], back_2[MOST:]], axis=0)

    ring = jnp.array([0, SIDE - 1, 1, 2], jnp.int32)
    ys, zs = (y + ring) % SIDE, (z + ring) % SIDE
    cols = jnp.concatenate([ys * 2 + c, ys * 2 + 1 - c])

    def table(d0, d1):
        xs = (x + jnp.array([d0, d1], jnp.int32)) % SIDE
        blocks = (xs[None, :] * SIDE + zs[:, None]).reshape(-1)
        return jnp.concatenate([cols, blocks, zs]).astype(jnp.int32)

    tab0, tab1 = table(0, 3), table(1, 2)

    a_near0, g_near0 = both(a0, "z"), both(g0, "y")
    a_near0, g_near0, a1, g1 = hold((a_near0, g_near0, a1, g1))
    a_far0, g_far0 = ring_far(*a_near0, "z"), ring_far(*g_near0, "y")
    a_far0, g_far0 = hold((a_far0, g_far0))
    s0, t0 = join_rows(a0, a_near0, a_far0), join_cols(g0, g_near0, g_far0)

    acts0 = lax.all_gather(s0, ("y", "c"), axis=0)
    near0, t0x = both(t0, "z"), swap(t0)
    g_near1 = both(g1, "y")
    g_near1, t0x, a1 = hold((g_near1, t0x, a1))
    g_far1 = ring_far(*g_near1, "y")
    g_far1, a1 = hold((g_far1, a1))
    t1 = join_cols(g1, g_near1, g_far1)
    a_near1 = both(a1, "z")
    near0, a_near1, t1 = hold((near0, a_near1, t1))
    far0, a_far1 = ring_far(*near0, "z"), ring_far(*a_near1, "z")
    far0, a_far1, t1 = hold((far0, a_far1, t1))
    s1 = join_rows(a1, a_near1, a_far1)
    acts1 = lax.all_gather(s1, ("y", "c"), axis=0)
    near1 = both(t1, "z")
    near0x, far0x = (swap(near0[0]), swap(near0[1])), (swap(far0[0]), swap(far0[1]))
    t1x = swap(t1)
    raw0, wg0 = raw_call(tab0, (t0, *near0, *far0, t0x, *near0x, *far0x), down_weight)
    near1, t1x, raw0 = hold((near1, t1x, raw0))
    far1, near1x = ring_far(*near1, "z"), (swap(near1[0]), swap(near1[1]))
    dup0, hid0, gg, sums0 = main_call(tab0, acts0, raw0, gate_pre, up_weight, None, True)
    far1, near1x, dup0, sums0 = hold((far1, near1x, dup0, sums0))
    sum0 = lax.psum_scatter(sums0, ("y", "c"), scatter_dimension=0, tiled=True)
    sum0 = lax.psum_scatter(sum0, "z", scatter_dimension=0, tiled=True)
    far1x = (swap(far1[0]), swap(far1[1]))
    raw1, wg1 = raw_call(tab1, (t1, *near1, *far1, t1x, *near1x, *far1x), down_weight)
    dup1, hid1, gg, mine1, other1 = main_call(tab1, acts1, raw1, gate_pre, up_weight, gg, False)
    got1 = swap(other1)
    grad_up = up_grad_call(acts0, acts1, dup0, dup1, 0, None)
    got1, grad_up = hold((got1, grad_up))
    sum1 = PlaneSum(mine1, got1)
    first1 = sum1.first()
    grad_up = up_grad_call(acts0, acts1, dup0, dup1, 1, grad_up)
    first1, grad_up = hold((first1, grad_up))
    second1 = sum1.second(first1)
    grad_down = down_grad_call(tab0, wg0, wg1, hid0, hid1)
    second1, grad_down = hold((second1, grad_down))
    sum1 = sum1.third(second1)
    sum1, sum0 = hold((sum1, sum0))

    home = jnp.concatenate(
        [
            sum0[:MOST],
            go(sum0[MOST:], "x", -1),
            go(sum1[MOST:], "x", 2),
            go(sum1[:MOST], "x", 1),
        ],
        axis=0,
    )
    own_input = mul(match, home, TN).astype(bf16)
    route = jnp.sum(home.astype(f32) * slot_acts.astype(f32), axis=1)
    route = jnp.where(used, route / jnp.where(used, weight, 1.0), 0.0).reshape(EXPERTS, MOST)
    token_route = jnp.sum(found.astype(f32) * route[:, :, None], axis=1).T
    terms = jnp.sum(token_route[:, None, :] * hit.astype(f32), axis=2)
    terms = terms + swap(terms)
    terms = (terms + go(terms, "y", 2)) + (go(terms, "y", 1) + go(terms, "y", -1))
    return (own_input, terms, grad_up, grad_down, gg)


def solution(mesh):
    grid = Mesh(mesh.devices.reshape(SIDE, SIDE, SIDE, 2), ("x", "z", "y", "c"))
    group, cuts, every = ("x", "z"), ("y", "c"), ("x", "z", "y", "c")
    return jax.shard_map(
        body,
        mesh=grid,
        in_specs=(
            P(group, cuts),
            P(group, cuts),
            P(group, None),
            P(group, None),
            P(None, every),
            P(None, every),
            P(every, None),
        ),
        out_specs=(
            P(group, cuts),
            P(group, None),
            P(None, every),
            P(every, None),
            P(None, every),
        ),
        check_vma=False,
    )
```

```python
import functools
import math

import jax
import jax.numpy as jnp
from jax import lax
from jax.experimental import pallas as pl
from jax.experimental.pallas import tpu as pltpu
from jax.sharding import Mesh
from jax.sharding import PartitionSpec as P

EXPERTS = 4
MOST = 80
SIDE = 4

bf16 = jnp.bfloat16
f32 = jnp.float32
hold = lax.optimization_barrier
root_coef = math.sqrt(2.0 / math.pi)


def gelu_pair(gate):
    inner = root_coef * (gate + 0.044715 * gate * gate * gate)
    tval = jnp.tanh(inner)
    act = 0.5 * gate * (1.0 + tval)
    slope = 0.5 * (1.0 + tval) + 0.5 * gate * (1.0 - tval * tval) * root_coef * (
        1.0 + 3.0 * 0.044715 * gate * gate
    )
    return (act, slope)


def go(v, axis, step):
    return lax.ppermute(v, axis, [(i, (i + step) % SIDE) for i in range(SIDE)])


def both(v, axis):
    return go(v, axis, 1), go(v, axis, -1)


def swap(v):
    return lax.ppermute(v, "c", [(0, 1), (1, 0)])


def add(*parts):
    total = parts[0].astype(f32)
    for part in parts[1:]:
        total = total + part.astype(f32)
    return total.astype(bf16)


def ring_far(left, right, axis):
    w = left.shape[1] // 2
    return go(left[:, :w], axis, 1), go(right[:, w:], axis, -1)


def join_rows(a, near, far):
    return jnp.concatenate([a, *near, jnp.concatenate(far, axis=1)], axis=0)


def join_cols(g, near, far):
    return jnp.concatenate([g, *near, *far], axis=1)


def cut(v, along):
    half = v.shape[along] // 2
    return (v[:half], v[half:]) if along == 0 else (v[:, :half], v[:, half:])


def widen(v, along, second):
    pads = [(0, 0), (0, 0)]
    pads[along] = (v.shape[along], 0) if second else (0, v.shape[along])
    return jnp.pad(v, pads)


def ring_all(own, left, right, opp, axis):
    return add(own, go(left, axis, -1), go(right, axis, 1), go(opp, axis, 2))


class PlaneSum:
    def __init__(self, mine, got):
        rows, cols = mine.shape
        self.n, k = rows // SIDE, cols // 2
        self.w = k // SIDE
        n, w = self.n, self.w

        def part(r0, r1, c0, c1):
            return mine[r0:r1, c0:c1], got[r0:r1, c0:c1]

        self.z = [part(i * n, (i + 1) * n, 0, k) for i in range(SIDE)]
        self.y = [part(0, rows, k + i * w, k + (i + 1) * w) for i in range(SIDE)]

    def first(self):
        za, zb = cut(add(*self.z[3]), 1)
        ya, yb = cut(add(*self.y[3]), 0)
        return go(za, "z", 1), go(zb, "z", -1), go(ya, "y", 1), go(yb, "y", -1)

    def second(self, met):
        za, zb, ya, yb = met
        return (
            go(add(*self.z[2], widen(za, 1, False)), "z", 1),
            go(add(*self.z[1], widen(zb, 1, True)), "z", -1),
            go(add(*self.y[2], widen(ya, 0, False)), "y", 1),
            go(add(*self.y[1], widen(yb, 0, True)), "y", -1),
        )

    def third(self, met):
        n, w = self.n, self.w
        one, two = add(*self.z[0], *met[:2]), add(*self.y[0], *met[2:])
        one = ring_all(*[one[:, i * w : (i + 1) * w] for i in range(SIDE)], "y")
        two = ring_all(*[two[i * n : (i + 1) * n] for i in range(SIDE)], "z")
        return jnp.concatenate([one, two], axis=1)


anyspec = pl.BlockSpec(memory_space=pl.ANY)
smem = pl.BlockSpec(memory_space=pltpu.SMEM)
dma = pltpu.SemaphoreType.DMA
sds = jax.ShapeDtypeStruct
NT = (((1,), (1,)), ((), ()))
TN = (((0,), (0,)), ((), ()))


def mul(a, b, dims):
    return lax.dot_general(a, b, dims, preferred_element_type=f32)


def params():
    return pltpu.CompilerParams(vmem_limit_bytes=56 * 2**20)


def cost(flops, moved):
    return pl.CostEstimate(flops=flops, bytes_accessed=moved, transcendentals=0)


FULL = ((0, 0, 4), (1, 0, 4), (2, 0, 4), (3, 0, 2), (3, 2, 2))
HALVES = tuple((z, c, 2) for z in range(SIDE) for c in (0, 2))


def expert_kernel(tab, *refs, first, whole, plan):
    k = 2 * len(plan)
    pieces, (down, acts, gate, up) = refs[:k], refs[k : k + 4]
    k += 4 if first else 5
    wg_o, dup_o, hid_o, gg_o = refs[k : k + 4]
    k += 4
    outs = refs[k : k + (1 if whole else 2)]
    k += len(outs)
    g_v, w_v, a_v, v_v, raw_v, up_v, gate_v, dup_v, hid_v, gg_v, o_v = refs[k : k + 11]
    s_g, s_w, s_a, s_v, s_gate, s_gg, s_out, s_o = refs[k + 11 :]
    copy = pltpu.make_async_copy
    rows, wide = g_v.shape
    n, half, blk = rows // SIDE, wide // 2, wide // 8
    w = blk // 2

    def gate_spot(i):
        return pl.ds(pl.multiple_of(tab[8 + i] * MOST, MOST), MOST)

    g_in = [
        [
            copy(
                pieces[ci * len(plan) + i],
                g_v.at[pl.ds(z * n, n), pl.ds(ci * half + c * blk, m * blk)],
                s_g.at[ci * len(plan) + i],
            )
            for i, (z, c, m) in enumerate(plan)
        ]
        for ci in range(2)
    ]
    w_in = [
        copy(down.at[:, pl.ds(pl.multiple_of(tab[q] * blk, blk), blk)], w_v.at[q], s_w.at[q])
        for q in range(8)
    ]
    a_in = [copy(acts.at[q], a_v.at[q], s_a.at[q]) for q in range(8)]
    v_in = [copy(up.at[pl.ds(q * blk, blk)], v_v.at[q], s_v.at[q]) for q in range(8)]
    gate_in = [
        copy(gate.at[gate_spot(i)], gate_v.at[pl.ds(i * MOST, MOST)], s_gate.at[i])
        for i in range(8)
    ]
    gg_out = [
        copy(gg_v.at[pl.ds(i * MOST, MOST)], gg_o.at[gate_spot(i)], s_gg.at[i]) for i in range(8)
    ]
    side = [
        copy(g_v.at[:, pl.ds(ci * half, half)], wg_o.at[:, pl.ds(ci * half, half)], s_out.at[ci])
        for ci in range(2)
    ]
    for q in range(8):
        a_in[q].start()
        v_in[q].start()
    for q in range(8):
        a_in[q].wait()
        v_in[q].wait()
        if q == 2:
            for ci in range(2):
                for cp in g_in[ci]:
                    cp.start()
                for r in range(4):
                    w_in[ci * 4 + r].start()
            for cp in gate_in:
                cp.start()
        part = jnp.dot(a_v[q], v_v[q], preferred_element_type=f32)
        if q == 0:
            up_v[...] = part
        else:
            up_v[...] += part
    for q in range(8):
        if q % 4 == 0:
            for cp in g_in[q // 4]:
                cp.wait()
            side[q // 4].start()
        w_in[q].wait()
        part = mul(g_v[:, q * blk : (q + 1) * blk], w_v[q], NT)
        if q == 0:
            raw_v[...] = part
        else:
            raw_v[...] += part
    for cp in gate_in:
        cp.wait()

    def middle(i, carry):
        at = pl.ds(pl.multiple_of(i * MOST, MOST), MOST)
        act, slope = gelu_pair(gate_v[at, :].astype(f32))
        upv = up_v[at, :]
        dhid = raw_v[at, :]
        hid_v[at, :] = (act * upv).astype(bf16)
        dup_v[at, :] = (dhid * act).astype(bf16)
        gg_v[at, :] = (dhid * upv * slope).astype(bf16)
        return carry

    lax.fori_loop(0, rows // MOST, middle, 0)
    more = gg_out + [copy(dup_v, dup_o, s_out.at[2]), copy(hid_v, hid_o, s_out.at[3])]
    for cp in more:
        cp.start()

    flying = [[], []]
    for turn, q in enumerate((4, 5, 6, 7, 0, 1, 2, 3)):
        slot = turn % 2
        for cp in flying[slot]:
            cp.wait()
        spot = tab[q]
        o_v[slot] = mul(dup_v[...], v_v[spot], NT).astype(bf16)
        if whole:
            flying[slot] = [
                copy(
                    o_v.at[slot, pl.ds(i * n, n)],
                    outs[0].at[pl.ds(pl.multiple_of((spot * SIDE + tab[16 + i]) * n, n), n)],
                    s_o.at[slot, i],
                )
                for i in range(SIDE)
            ]
        else:
            flying[slot] = [
                copy(
                    o_v.at[slot, :, pl.ds(h * w, w)],
                    outs[0 if q < 4 else 1].at[:, pl.ds(h * 4 * w + q % 4 * w, w)],
                    s_o.at[slot, h],
                )
                for h in range(2)
            ]
        for cp in flying[slot]:
            cp.start()
    for cp in flying[0] + flying[1] + side + more:
        cp.wait()


def expert_call(tab, pieces, down, acts, gate, up, gg, whole, plan):
    wide, deep = up.shape
    rows, blk = acts.shape[1:]
    first = gg is None
    ins = [tab, *pieces, down, acts, gate, up] + ([] if first else [gg])
    small = sds((rows, deep), bf16)
    sums = (
        (sds((rows * 8, blk), bf16),)
        if whole
        else (sds((rows, wide // 2), bf16), sds((rows, wide // 2), bf16))
    )
    return pl.pallas_call(
        functools.partial(expert_kernel, first=first, whole=whole, plan=plan),
        out_shape=(sds((rows, wide), bf16), small, small, sds(gate.shape, bf16)) + sums,
        in_specs=[smem] + [anyspec] * (len(ins) - 1),
        out_specs=(anyspec,) * (4 + len(sums)),
        scratch_shapes=[
            pltpu.VMEM((rows, wide), bf16),
            pltpu.VMEM((8, deep, blk), bf16),
            pltpu.VMEM((8, rows, blk), bf16),
            pltpu.VMEM((8, blk, deep), bf16),
            pltpu.VMEM((rows, deep), f32),
            pltpu.VMEM((rows, deep), f32),
            pltpu.VMEM((rows, deep), bf16),
            pltpu.VMEM((rows, deep), bf16),
            pltpu.VMEM((rows, deep), bf16),
            pltpu.VMEM((rows, deep), bf16),
            pltpu.VMEM((2, rows, blk), bf16),
            dma((16,)),
            dma((8,)),
            dma((8,)),
            dma((8,)),
            dma((8,)),
            dma((8,)),
            dma((4,)),
            dma((2, 4)),
        ],
        input_output_aliases={} if first else {len(ins) - 1: 3},
        compiler_params=params(),
        cost_estimate=cost(6 * rows * wide * deep, 2 * (3 * rows * wide + 2 * wide * deep)),
        name="expert_rows",
    )(*ins)


def grad_kernel(*refs, turns, first, up):
    tab, r0, r1, f0, f1 = refs[:5]
    out, r_v, f_v, o_v, s_r, s_f, s_o = refs[5 if first else 6 :]
    copy = pltpu.make_async_copy
    rows = f0.shape[0]
    blk = r_v.shape[2]

    def loads(i):
        q = turns[i]
        return [
            copy(
                src.at[q] if up else src.at[:, pl.ds(q * blk, blk)],
                r_v.at[i % 3, pl.ds(j * rows, rows)],
                s_r.at[i % 3, j],
            )
            for j, src in enumerate((r0, r1))
        ]

    def store(i):
        q = turns[i]
        if up:
            to = out.at[pl.ds(q * blk, blk)]
        else:
            to = out.at[:, pl.ds(pl.multiple_of(tab[q] * blk, blk), blk)]
        return copy(o_v.at[i % 2], to, s_o.at[i % 2])

    count = len(turns)
    fixed = [copy(f, f_v.at[pl.ds(j * rows, rows)], s_f.at[j]) for j, f in enumerate((f0, f1))]
    ahead, outs = [loads(i) for i in range(count)], [store(i) for i in range(count)]
    for cp in fixed + ahead[0] + ahead[1]:
        cp.start()
    for cp in fixed:
        cp.wait()
    for i in range(count):
        for cp in ahead[i]:
            cp.wait()
        if i + 2 < count:
            for cp in ahead[i + 2]:
                cp.start()
        if i >= 2:
            outs[i - 2].wait()
        if up:
            o_v[i % 2] = mul(r_v[i % 3], f_v[...], TN).astype(bf16)
        else:
            o_v[i % 2] = mul(f_v[...], r_v[i % 3], TN).astype(bf16)
        outs[i].start()
    outs[count - 2].wait()
    outs[count - 1].wait()


def grad_call(tab, r0, r1, f0, f1, turns, into, up):
    rows, deep = f0.shape
    blk = r0.shape[2] if up else r0.shape[1] // 8
    first = into is None
    ins = [tab, r0, r1, f0, f1] + ([] if first else [into])
    return pl.pallas_call(
        functools.partial(grad_kernel, turns=turns, first=first, up=up),
        out_shape=sds((8 * blk, deep) if up else (deep, 8 * blk), bf16),
        in_specs=[smem] + [anyspec] * (len(ins) - 1),
        out_specs=anyspec,
        scratch_shapes=[
            pltpu.VMEM((3, 2 * rows, blk), bf16),
            pltpu.VMEM((2 * rows, deep), bf16),
            pltpu.VMEM((2, blk, deep) if up else (2, deep, blk), bf16),
            dma((3, 2)),
            dma((2,)),
            dma((2,)),
        ],
        input_output_aliases={} if first else {5: 0},
        compiler_params=params(),
        cost_estimate=cost(4 * rows * blk * deep * len(turns), 4 * rows * blk * len(turns)),
        name="up_grad" if up else "down_grad",
    )(*ins)


def body(acts, grad_out, expert_ids, combine, gate_pre, up_weight, down_weight):
    x, z, y, c = (lax.axis_index(name) for name in ("x", "z", "y", "c"))
    rel = jnp.arange(EXPERTS, dtype=jnp.int32)
    hit = expert_ids[:, :, None] == (x + rel) % EXPERTS
    member = jnp.any(hit, axis=1)
    wtab = jnp.sum(combine[:, :, None] * hit.astype(f32), axis=1)
    count = member.astype(jnp.int32)
    rank = jnp.cumsum(count, axis=0) - count
    places = jnp.arange(MOST, dtype=jnp.int32)
    found = member.T[:, None, :] & (rank.T[:, None, :] == places[None, :, None])
    match = found.astype(bf16).reshape(EXPERTS * MOST, -1)
    weight = jnp.sum(found.astype(f32) * wtab.T[:, None, :], axis=2).reshape(-1)
    used = jnp.any(found, axis=2).reshape(-1)

    slot_acts = jnp.dot(match, acts, preferred_element_type=f32).astype(bf16)
    slot_grad = jnp.dot(match, grad_out, preferred_element_type=f32)
    slot_wgrad = (weight[:, None] * slot_grad).astype(bf16)

    def send(k, step):
        rows = slice(k * MOST, (k + 1) * MOST)
        return go(jnp.concatenate([slot_acts[rows], slot_wgrad[rows]], axis=0), "x", step)

    back_1 = send(1, 1)
    back_3 = send(3, -1)
    back_2 = send(2, 2)
    a0 = jnp.concatenate([slot_acts[:MOST], back_1[:MOST]], axis=0)
    g0 = jnp.concatenate([slot_wgrad[:MOST], back_1[MOST:]], axis=0)
    a1 = jnp.concatenate([back_3[:MOST], back_2[:MOST]], axis=0)
    g1 = jnp.concatenate([back_3[MOST:], back_2[MOST:]], axis=0)

    ring = jnp.array([0, SIDE - 1, 1, 2], jnp.int32)
    ys, zs = (y + ring) % SIDE, (z + ring) % SIDE
    cols = jnp.concatenate([ys * 2 + c, ys * 2 + 1 - c])

    def table(d0, d1):
        xs = (x + jnp.array([d0, d1], jnp.int32)) % SIDE
        blocks = (xs[None, :] * SIDE + zs[:, None]).reshape(-1)
        return jnp.concatenate([cols, blocks, zs]).astype(jnp.int32)

    tab0, tab1 = table(0, 3), table(1, 2)

    a_near0, g_near0 = both(a0, "z"), both(g0, "y")
    a_near0, g_near0, a1, g1 = hold((a_near0, g_near0, a1, g1))
    a_far0, g_far0 = ring_far(*a_near0, "z"), ring_far(*g_near0, "y")
    a_far0, g_far0 = hold((a_far0, g_far0))
    s0, t0 = join_rows(a0, a_near0, a_far0), join_cols(g0, g_near0, g_far0)

    def swaps(vs):
        return tuple(swap(v) for v in vs)

    acts0 = lax.all_gather(s0, ("y", "c"), axis=0)
    near0, t0x = both(t0, "z"), swap(t0)
    g_near1 = both(g1, "y")
    g_near1, t0x, a1 = hold((g_near1, t0x, a1))
    g_far1 = ring_far(*g_near1, "y")
    g_far1, a1 = hold((g_far1, a1))
    own1 = (
        jnp.concatenate([g1, g_near1[0]], axis=1),
        jnp.concatenate([g_near1[1], *g_far1], axis=1),
    )
    a_near1 = both(a1, "z")
    near0, a_near1, own1 = hold((near0, a_near1, own1))
    far0, a_far1 = ring_far(*near0, "z"), ring_far(*a_near1, "z")
    far0, a_far1, own1 = hold((far0, a_far1, own1))
    s1 = join_rows(a1, a_near1, a_far1)
    acts1 = lax.all_gather(s1, ("y", "c"), axis=0)
    fore1 = go(own1[0], "z", 1), go(own1[1], "z", -1)
    near0x, far0x, own1x = swaps(near0), swaps(far0), swaps(own1)
    fore1, near0x, far0x, own1x, acts0 = hold((fore1, near0x, far0x, own1x, acts0))
    last1 = go(own1[1], "z", 1), go(own1[0], "z", -1), go(fore1[0], "z", 1), go(fore1[1], "z", -1)
    wg0, dup0, hid0, gg, sums0 = expert_call(
        tab0, (t0, *near0, *far0, t0x, *near0x, *far0x),
        down_weight, acts0, gate_pre, up_weight, None, True, FULL,
    )
    last1, dup0, sums0 = hold((last1, dup0, sums0))
    sum0 = lax.psum_scatter(sums0, ("y", "c"), scatter_dimension=0, tiled=True)
    sum0 = lax.psum_scatter(sum0, "z", scatter_dimension=0, tiled=True)

    def order(own, fore, last):
        return (*own, fore[0], last[0], last[1], fore[1], last[2], last[3])

    wg1, dup1, hid1, gg, mine1, other1 = expert_call(
        tab1, order(own1, fore1, last1) + order(own1x, swaps(fore1), swaps(last1)),
        down_weight, acts1, gate_pre, up_weight, gg, False, HALVES,
    )
    got1 = swap(other1)
    grad_up = grad_call(tab0, acts0, acts1, dup0, dup1, range(4), None, True)
    got1, grad_up = hold((got1, grad_up))
    sum1 = PlaneSum(mine1, got1)
    first1 = sum1.first()
    grad_up = grad_call(tab0, acts0, acts1, dup0, dup1, range(4, 8), grad_up, True)
    first1, grad_up = hold((first1, grad_up))
    second1 = sum1.second(first1)
    grad_down = grad_call(tab0, wg0, wg1, hid0, hid1, range(6), None, False)
    second1, grad_down = hold((second1, grad_down))
    sum1 = sum1.third(second1)
    sum1, sum0, grad_down = hold((sum1, sum0, grad_down))
    grad_down = grad_call(tab0, wg0, wg1, hid0, hid1, range(6, 8), grad_down, False)

    home = jnp.concatenate(
        [
            sum0[:MOST],
            go(sum0[MOST:], "x", -1),
            go(sum1[MOST:], "x", 2),
            go(sum1[:MOST], "x", 1),
        ],
        axis=0,
    )
    home, grad_down = hold((home, grad_down))
    own_input = mul(match, home, TN).astype(bf16)
    route = jnp.sum(home.astype(f32) * slot_acts.astype(f32), axis=1)
    route = jnp.where(used, route / jnp.where(used, weight, 1.0), 0.0).reshape(EXPERTS, MOST)
    token_route = jnp.sum(found.astype(f32) * route[:, :, None], axis=1).T
    terms = jnp.sum(token_route[:, None, :] * hit.astype(f32), axis=2)
    terms = terms + swap(terms)
    terms = (terms + go(terms, "y", 2)) + (go(terms, "y", 1) + go(terms, "y", -1))
    return (own_input, terms, grad_up, grad_down, gg)


def solution(mesh):
    grid = Mesh(mesh.devices.reshape(SIDE, SIDE, SIDE, 2), ("x", "z", "y", "c"))
    group, cuts, every = ("x", "z"), ("y", "c"), ("x", "z", "y", "c")
    return jax.shard_map(
        body,
        mesh=grid,
        in_specs=(
            P(group, cuts),
            P(group, cuts),
            P(group, None),
            P(group, None),
            P(None, every),
            P(None, every),
            P(every, None),
        ),
        out_specs=(
            P(group, cuts),
            P(group, None),
            P(None, every),
            P(every, None),
            P(None, every),
        ),
        check_vma=False,
    )
```
